32 devices in a mesh: expert: 4 (over y, x), fsdp: 8 (over z, core).
Axes of the slice: x: 2, y: 2, z: 4, core: 2. Of those that a mesh axis runs over, the one named last changes fastest.
Arguments:
- tokens: bfloat16 [512, 3072], P('expert'), may hold values from -6 to 6
- assignment: int32 [512, 2], P('expert'), may hold values from 0 to 3, all different within a row; in each aligned block of 128 rows (0 to 127, 128 to 255, ...) at most 96 rows name the same one
- route_weight: float32 [512, 2], P('expert'), may hold values from 0.25 to 1
- cotangent: bfloat16 [512, 3072], P('expert'), may hold values from -6 to 6
- w_gate: bfloat16 [4, 3072, 8192], P('expert', None, 'fsdp'), may hold values from -0.109375 to 0.109375
- w_up: bfloat16 [4, 3072, 8192], P('expert', None, 'fsdp'), may hold values from -0.109375 to 0.109375
- w_down: bfloat16 [4, 8192, 3072], P('expert', 'fsdp'), may hold values from -0.0625 to 0.0625
Outputs:
- moe_out: bfloat16 [512, 3072], P('expert')
- grad_tokens: bfloat16 [512, 3072], P('expert')
- grad_prob: float32 [512, 2], P('expert')
- grad_gate: bfloat16 [4, 3072, 8192], P('expert', None, 'fsdp')
- grad_up: bfloat16 [4, 3072, 8192], P('expert', None, 'fsdp')
- grad_down: bfloat16 [4, 8192, 3072], P('expert', 'fsdp')
The draws below stay inside these ranges and needn't reach their ends.
Inputs may be any that keep to these rules, and one draw needn't show every extreme that they name: `assignment`: each token names two different experts. Among the 128 tokens of one block no expert is named more than 96 times, and in some block some expert is named exactly 96 times.
All inputs are finite; a program needn't handle non-finite values.
Results may differ from the reference program's by a relative error of at most 0.02.
Values may be sent and summed in bfloat16 or wider, within the bound.
No kernel may reach another device: no remote copies, remote signals or barrier semaphores. Data moves between devices by JAX's collectives and lax.ppermute only.
A program may use at most 128 MiB of HBM per device.

```python
import math
import jax
import jax.numpy as jnp
import numpy as np
from jax import lax

D = 3072
FF = 8192
TOK_DEV = 128
E = 4
CAP = 96
TOKENS = 512
N_FSDP = 8


def level_of(stream_key, extent, shards, smallest, high):
    level = 1.0
    for dim, blocks in shards:
        draws = jax.random.uniform(jax.random.fold_in(jax.random.fold_in(stream_key, 6), dim), (blocks,), jnp.float32, smallest / len(shards), high / len(shards))
        level = level * jnp.repeat(jnp.exp(draws), extent[dim] // blocks).reshape((-1,) + (1,) * (len(extent) - 1 - dim))
    return level


def deal_out(stream_key, own, number, rows, count, top, most, skew):
    order = jax.random.permutation(stream_key, count)
    crowded, usual = load_shares(count, rows * top, most, skew, True), load_shares(count, rows * top, most, skew, False)
    places = jnp.arange(count)

    def named(tallies, turn):
        used = int((tallies > 0).sum())
        fixed = max(1, used // 4)
        moved = fixed + (places - fixed + turn * (used - fixed)) % max(1, count - fixed)
        return jnp.zeros((count,), jnp.int32).at[order[jnp.where(places < fixed, places, moved)]].set(jnp.asarray(tallies, jnp.int32))

    tallies = jnp.where(number % 4 == 0, named(crowded, number // 4), named(usual, number - number // 4 - 1))
    mixed = jax.random.permutation(jax.random.fold_in(own, 3), count)
    giver, taker = mixed[0:count // 2 * 2:2], mixed[1:count // 2 * 2:2]
    room = jnp.minimum(tallies[giver] - 1, most - tallies[taker]) // 2
    room = jnp.where((giver == order[0]) | (taker == order[0]) | (tallies[taker] == 0), 0, jnp.maximum(room, 0))
    moved = jax.random.randint(jax.random.fold_in(own, 4), (count // 2,), 0, 1 << 20) % (room + 1)
    tallies = tallies.at[giver].add(-moved).at[taker].add(moved)
    members = jnp.searchsorted(jnp.cumsum(tallies), jnp.arange(rows * top), side="right").astype(jnp.int32)
    grid = members.reshape(top, rows).T
    grid = grid[jax.random.permutation(jax.random.fold_in(own, 1), rows)]
    turn = jax.random.randint(jax.random.fold_in(own, 2), (rows, 1), 0, top)
    return jnp.take_along_axis(grid, (jnp.arange(top)[None, :] + turn) % top, axis=1)


def load_shares(amount, total, most, skew, full):
    portions = [(1 << 20) // math.isqrt(grade ** skew) + 1 for grade in range(1, amount + 1)]
    largest = most if full else min(most, max(-(-total // amount), total * portions[0] // sum(portions)))
    least = 1 if total - largest >= amount - 1 else 0
    holding, spare = [largest] + [least] * (amount - 1), total - largest - least * (amount - 1)
    while spare > 0:
        free = [i for i in range(1, amount) if holding[i] < largest] or [i for i in range(1, amount) if holding[i] < most]
        whole, remaining = sum([portions[i] for i in free]), spare
        for i in free:
            addition = min(most - holding[i], max(1, remaining * portions[i] // whole), spare)
            holding[i] = holding[i] + addition
            spare = spare - addition
    return np.array(holding)


def bell_draw(own_key, shape, scale, most, pieces=(), held_as=jnp.bfloat16):
    level = level_of(own_key, shape, pieces, -0.22, 0.18) if pieces else 1.0
    values = jax.random.normal(own_key, shape, jnp.float32) * scale * level
    return jnp.minimum(jnp.maximum(values, -most), most).astype(held_as)


def setup_inputs(seed: int = 0) -> dict:
    streams_of = jax.random.split(jax.random.key(seed), 8)
    tokens = bell_draw(streams_of[0], (TOKENS, D), 1.0, 6.0, ((0, 4),))
    assignment_keys = jax.random.split(jax.random.fold_in(streams_of[1], 1), TOKENS // TOK_DEV)
    assignment_turns = jax.random.permutation(jax.random.fold_in(streams_of[1], 3), TOKENS // TOK_DEV)
    assignment = jax.vmap(lambda own, number: deal_out(jax.random.fold_in(streams_of[1], 2), own, number, TOK_DEV, E, 2, CAP, 2))(assignment_keys, assignment_turns).reshape((TOKENS, 2))
    route_weight = jnp.clip(0.25 + 0.75 * jax.random.uniform(streams_of[2], (TOKENS, 2), jnp.float32) ** level_of(streams_of[2], (TOKENS, 2), ((0, 4),), -0.2, 0.2), 0.25, 1.0)
    cotangent = bell_draw(streams_of[3], (TOKENS, D), 1.0, 6.0, ((0, 4),))
    w_gate = bell_draw(streams_of[4], (E, D, FF), D ** -0.5, 0.109375, ((0, 4), (2, 8)))
    w_up = bell_draw(streams_of[5], (E, D, FF), D ** -0.5, 0.109375, ((0, 4), (2, 8)))
    w_down = bell_draw(streams_of[6], (E, FF, D), FF ** -0.5, 0.0625, ((0, 4), (1, 8)))
    return dict(tokens=tokens, assignment=assignment, route_weight=route_weight, cotangent=cotangent, w_gate=w_gate, w_up=w_up, w_down=w_down)


def slot_table(assignment):
    flat = assignment.reshape(-1)
    onehot = (flat[:, None] == jnp.arange(E, dtype=jnp.int32)[None, :]).astype(jnp.int32)
    before = jnp.cumsum(onehot, axis=0) - onehot
    position = jnp.sum(before * onehot, axis=1).astype(jnp.int32)
    return (flat * CAP + position).astype(jnp.int32).reshape(assignment.shape)


def rounded(value):
    return lax.optimization_barrier(value.astype(jnp.bfloat16)).astype(jnp.float32)


def piece_sums(term, rows):
    def step(total, index):
        return total + rounded(term(index)), None

    start = jnp.zeros((rows, D), jnp.float32)
    total, _ = lax.scan(step, start, jnp.arange(N_FSDP, dtype=jnp.int32))
    return total.astype(jnp.bfloat16)


def expert_pass(rows_x, rows_dy, gate_mat, up_mat, down_mat):
    piece = FF // N_FSDP
    rows = rows_x.shape[0]
    pre_gate = jnp.dot(rows_x, gate_mat, preferred_element_type=jnp.float32)
    pre_up = jnp.dot(rows_x, up_mat, preferred_element_type=jnp.float32)
    sigma = jax.nn.sigmoid(pre_gate)
    silu_gate = pre_gate * sigma
    hidden = (silu_gate * pre_up).astype(jnp.bfloat16)

    def out_term(index):
        part = lax.dynamic_slice_in_dim(hidden, index * piece, piece, 1)
        down_part = lax.dynamic_slice_in_dim(down_mat, index * piece, piece, 0)
        return jnp.dot(part, down_part, preferred_element_type=jnp.float32)

    expert_out = piece_sums(out_term, rows)
    grad_hidden = jnp.dot(rows_dy, down_mat.T, preferred_element_type=jnp.float32)
    grad_down = jnp.dot(hidden.T, rows_dy, preferred_element_type=jnp.float32).astype(jnp.bfloat16)
    grad_pre_gate = (grad_hidden * pre_up * sigma * (1.0 + pre_gate * (1.0 - sigma))).astype(jnp.bfloat16)
    grad_pre_up = (grad_hidden * silu_gate).astype(jnp.bfloat16)
    grad_gate = jnp.dot(rows_x.T, grad_pre_gate, preferred_element_type=jnp.float32).astype(jnp.bfloat16)
    grad_up = jnp.dot(rows_x.T, grad_pre_up, preferred_element_type=jnp.float32).astype(jnp.bfloat16)

    def back_term(index):
        gate_part = lax.dynamic_slice_in_dim(grad_pre_gate, index * piece, piece, 1)
        up_part = lax.dynamic_slice_in_dim(grad_pre_up, index * piece, piece, 1)
        gate_cols = lax.dynamic_slice_in_dim(gate_mat, index * piece, piece, 1)
        up_cols = lax.dynamic_slice_in_dim(up_mat, index * piece, piece, 1)
        return (jnp.dot(gate_part, gate_cols.T, preferred_element_type=jnp.float32)
                + jnp.dot(up_part, up_cols.T, preferred_element_type=jnp.float32))

    slot_grad = piece_sums(back_term, rows)
    return expert_out, slot_grad, grad_gate, grad_up, grad_down


def reference(tokens, assignment, route_weight, cotangent, w_gate, w_up, w_down):
    blocks = TOKENS // TOK_DEV
    slot_count = E * CAP
    table = jax.vmap(slot_table)(assignment.reshape(blocks, TOK_DEV, 2))
    block_ids = jnp.broadcast_to(jnp.arange(blocks, dtype=jnp.int32)[:, None, None], table.shape)
    rows_in = jnp.broadcast_to(tokens.reshape(blocks, TOK_DEV, 1, D), (blocks, TOK_DEV, 2, D))
    sent_tokens = jnp.zeros((blocks, slot_count, D), jnp.bfloat16).at[block_ids, table].set(rows_in)
    weights3 = route_weight.reshape(blocks, TOK_DEV, 2)
    cot_f = cotangent.reshape(blocks, TOK_DEV, 1, D).astype(jnp.float32)
    weighted = (weights3[..., None] * cot_f).astype(jnp.bfloat16)
    sent_cot = jnp.zeros((blocks, slot_count, D), jnp.bfloat16).at[block_ids, table].set(weighted)
    out_list, grad_list, gate_list, up_list, down_list = [], [], [], [], []
    for expert in range(E):
        rows_x = sent_tokens[:, expert * CAP:(expert + 1) * CAP].reshape(-1, D)
        rows_dy = sent_cot[:, expert * CAP:(expert + 1) * CAP].reshape(-1, D)
        result = expert_pass(rows_x, rows_dy, w_gate[expert], w_up[expert], w_down[expert])
        out_list.append(result[0].reshape(blocks, CAP, D))
        grad_list.append(result[1].reshape(blocks, CAP, D))
        gate_list.append(result[2])
        up_list.append(result[3])
        down_list.append(result[4])
    out_slots = jnp.concatenate(out_list, axis=1)
    grad_slots = jnp.concatenate(grad_list, axis=1)
    route_out = out_slots[block_ids, table].astype(jnp.float32)
    route_grad = grad_slots[block_ids, table].astype(jnp.float32)
    moe_out = jnp.sum(weights3[..., None] * route_out, axis=2).astype(jnp.bfloat16).reshape(TOKENS, D)
    grad_prob = jnp.sum(cot_f * route_out, axis=3).reshape(TOKENS, 2)
    grad_tokens = jnp.sum(route_grad, axis=2).astype(jnp.bfloat16).reshape(TOKENS, D)
    return (moe_out, grad_tokens, grad_prob, jnp.stack(gate_list), jnp.stack(up_list), jnp.stack(down_list))
```

```python
import jax
import jax.numpy as jnp
from jax import lax
from jax.sharding import PartitionSpec as P

AXES = ("expert", "fsdp")


def log2(size):
    return size.bit_length() - 1


def swap(value, groups, shards, partner):
    pairs = []
    for e in range(groups):
        for f in range(shards):
            to_e, to_f = partner(e, f)
            pairs.append((e * shards + f, to_e * shards + to_f))
    return lax.ppermute(value, AXES, pairs)


class Links:
    def __init__(self):
        self.groups = lax.axis_size("expert")
        self.shards = lax.axis_size("fsdp")
        self.steps = log2(self.groups)
        self.expert = lax.axis_index("expert")
        fsdp = lax.axis_index("fsdp")
        self.core = fsdp % 2
        self.deep = (fsdp // 2) % 2

    def order(self, core):
        return [(k + core) % self.steps for k in range(self.steps)]

    def offsets(self, core):
        found = [0]
        for bit in self.order(core):
            found = found + [o ^ (1 << bit) for o in found]
        return found

    def to_core(self, value):
        return swap(value, self.groups, self.shards, lambda e, f: (e, f ^ 1))

    def to_expert(self, value, step):
        orders = [self.order(0), self.order(1)]
        return swap(
            value, self.groups, self.shards, lambda e, f: (e ^ (1 << orders[f % 2][step]), f)
        )

    def to_offset(self, value, offset):
        return swap(value, self.groups, self.shards, lambda e, f: (e ^ offset, f))

    def to_shard(self, value, bit):
        return swap(value, self.groups, self.shards, lambda e, f: (e, f ^ (1 << bit)))


def add(left, right):
    return (left.astype(jnp.float32) + right.astype(jnp.float32)).astype(jnp.bfloat16)


def gather_rows(links, rows):
    half = rows.shape[0] // 2
    own = lax.dynamic_slice_in_dim(rows, links.core * half, half, 0)
    rest = lax.dynamic_slice_in_dim(rows, (1 - links.core) * half, half, 0)
    held = own
    for step in range(links.steps):
        held = jnp.concatenate([held, links.to_expert(held, step)], axis=0)
    other = links.to_core(held[half:])
    return jnp.concatenate([held, rest, other], axis=0)


def order_rows(links, per_offset):
    half = per_offset.shape[1] // 2
    low = jnp.concatenate([per_offset[o, :half] for o in links.offsets(0)])
    high = jnp.concatenate([per_offset[o, half:] for o in links.offsets(1)])
    return jnp.where(
        links.core == 0, jnp.concatenate([low, high]), jnp.concatenate([high, low])
    )


def sum_rows(links, terms):
    middle = terms.shape[0] // 2
    held = add(terms[:middle], links.to_core(terms[middle:]))
    for step in reversed(range(links.steps)):
        count = held.shape[0] // 2
        held = add(held[:count], links.to_expert(held[count:], step))
    quarter = held.shape[0] // 2
    mine = lax.dynamic_slice_in_dim(held, links.deep * quarter, quarter, 0)
    theirs = lax.dynamic_slice_in_dim(held, (1 - links.deep) * quarter, quarter, 0)
    mine = add(mine, links.to_shard(theirs, 1))
    for bit in range(2, log2(links.shards)):
        mine = add(mine, links.to_shard(mine, bit))
    theirs = links.to_shard(mine, 1)
    part = jnp.where(
        links.deep == 0,
        jnp.concatenate([mine, theirs], axis=0),
        jnp.concatenate([theirs, mine], axis=0),
    )
    other = links.to_core(part)
    return jnp.where(
        links.core == 0,
        jnp.concatenate([part, other], axis=0),
        jnp.concatenate([other, part], axis=0),
    )


def per_device(tokens, assignment, route_weight, cotangent, w_gate, w_up, w_down):
    links = Links()
    width = tokens.shape[1]
    groups = links.groups
    gate_local, up_local, down_local = w_gate[0], w_up[0], w_down[0]

    received = []
    for offset in range(groups):
        there = links.expert ^ offset
        column = jnp.sum(jnp.where(assignment == there, route_weight, 0.0), axis=1)
        received.append(column if offset == 0 else links.to_offset(column, offset))
    weight = order_rows(links, jnp.stack(received))[:, None]

    rows_x = gather_rows(links, tokens)
    rows_c = gather_rows(links, cotangent)

    pre_gate = jnp.dot(rows_x, gate_local, preferred_element_type=jnp.float32)
    pre_up = jnp.dot(rows_x, up_local, preferred_element_type=jnp.float32)
    sigma = jax.nn.sigmoid(pre_gate)
    silu_gate = pre_gate * sigma
    hidden = silu_gate * pre_up
    scaled = (weight * hidden).astype(jnp.bfloat16)
    out_terms = jnp.dot(scaled, down_local, preferred_element_type=jnp.float32).astype(
        jnp.bfloat16
    )
    moe_out = sum_rows(links, out_terms)

    raw_hidden = jnp.dot(rows_c, down_local.T, preferred_element_type=jnp.float32)
    prob_term = jnp.sum(hidden * raw_hidden, axis=1, keepdims=True)
    lane = lax.broadcasted_iota(jnp.int32, (1, 128), 1)
    prob_terms = jnp.where(lane == links.expert, prob_term, 0.0).astype(jnp.bfloat16)
    grad_hidden = raw_hidden * weight
    grad_pre_gate = (grad_hidden * pre_up * sigma * (1.0 + pre_gate * (1.0 - sigma))).astype(
        jnp.bfloat16
    )
    grad_pre_up = (grad_hidden * silu_gate).astype(jnp.bfloat16)
    back_terms = (
        jnp.dot(grad_pre_gate, gate_local.T, preferred_element_type=jnp.float32)
        + jnp.dot(grad_pre_up, up_local.T, preferred_element_type=jnp.float32)
    ).astype(jnp.bfloat16)
    back = sum_rows(links, jnp.concatenate([back_terms, prob_terms], axis=1))
    grad_tokens = back[:, :width]
    prob_all = back[:, width:].astype(jnp.float32)
    grad_prob = jnp.stack(
        [
            jnp.sum(jnp.where(lane == assignment[:, k : k + 1], prob_all, 0.0), axis=1)
            for k in range(assignment.shape[1])
        ],
        axis=1,
    )

    grad_down = jnp.dot(scaled.T, rows_c, preferred_element_type=jnp.float32).astype(jnp.bfloat16)
    grad_gate = jnp.dot(rows_x.T, grad_pre_gate, preferred_element_type=jnp.float32).astype(
        jnp.bfloat16
    )
    grad_up = jnp.dot(rows_x.T, grad_pre_up, preferred_element_type=jnp.float32).astype(
        jnp.bfloat16
    )
    return (moe_out, grad_tokens, grad_prob, grad_gate[None], grad_up[None], grad_down[None])


def solution(mesh):
    return jax.shard_map(
        per_device,
        mesh=mesh,
        in_specs=(
            P("expert", None),
            P("expert", None),
            P("expert", None),
            P("expert", None),
            P("expert", None, "fsdp"),
            P("expert", None, "fsdp"),
            P("expert", "fsdp", None),
        ),
        out_specs=(
            P("expert", None),
            P("expert", None),
            P("expert", None),
            P("expert", None, "fsdp"),
            P("expert", None, "fsdp"),
            P("expert", "fsdp", None),
        ),
        check_vma=False,
    )
```

```python
import jax
import jax.numpy as jnp
from jax import lax
from jax.experimental import pallas as pl
from jax.experimental.pallas import tpu as pltpu
from jax.sharding import PartitionSpec as P

AXES = ("expert", "fsdp")
LANES = 128
BF = jnp.bfloat16
F32 = jnp.float32


def log2(size):
    return size.bit_length() - 1


def tile_of(size, most):
    tile = most
    while size % tile:
        tile -= LANES
    return tile


def swap(value, groups, shards, partner):
    pairs = []
    for e in range(groups):
        for f in range(shards):
            to_e, to_f = partner(e, f)
            pairs.append((e * shards + f, to_e * shards + to_f))
    return lax.ppermute(value, AXES, pairs)


class Links:
    def __init__(self):
        self.groups = lax.axis_size("expert")
        self.shards = lax.axis_size("fsdp")
        self.steps = log2(self.groups)
        self.expert = lax.axis_index("expert")
        fsdp = lax.axis_index("fsdp")
        self.core = fsdp % 2
        self.deep = (fsdp // 2) % 2

    def order(self, core):
        return [(k + core) % self.steps for k in range(self.steps)]

    def offsets(self, core):
        found = [0]
        for bit in self.order(core):
            found = found + [o ^ (1 << bit) for o in found]
        return found

    def to_core(self, value):
        return swap(value, self.groups, self.shards, lambda e, f: (e, f ^ 1))

    def to_expert(self, value, step):
        orders = [self.order(0), self.order(1)]
        return swap(
            value, self.groups, self.shards, lambda e, f: (e ^ (1 << orders[f % 2][step]), f)
        )

    def to_offset(self, value, offset):
        return swap(value, self.groups, self.shards, lambda e, f: (e ^ offset, f))

    def to_shard(self, value, bit):
        return swap(value, self.groups, self.shards, lambda e, f: (e, f ^ (1 << bit)))


def add(left, right):
    return (left.astype(F32) + right.astype(F32)).astype(BF)


def hold(value, *others):
    return lax.optimization_barrier((value, *others))[0]


def halves(links, rows):
    quarter = rows.shape[0] // 4
    found = []
    for core in (links.core, 1 - links.core):
        parts = [
            lax.dynamic_slice_in_dim(rows, (2 * core + deep) * quarter, quarter, 0)
            for deep in (links.deep, 1 - links.deep)
        ]
        found.append(jnp.concatenate(parts, axis=0))
    return found


def order_rows(links, per_offset):
    half, quarter = per_offset.shape[1] // 2, per_offset.shape[1] // 4
    parts = per_offset.reshape(links.groups, 2, 2, quarter)
    parts = jnp.where(links.deep == 0, parts, parts[:, :, ::-1]).reshape(links.groups, 2, half)
    middle = links.groups // 2
    chunks = []
    for part in (slice(0, middle), slice(middle, None)):
        low = jnp.concatenate([parts[o, 0] for o in links.offsets(0)[part]])
        high = jnp.concatenate([parts[o, 1] for o in links.offsets(1)[part]])
        chunks.append(
            jnp.where(
                links.core == 0, jnp.concatenate([low, high]), jnp.concatenate([high, low])
            )[:, None]
        )
    return chunks


def gather_tokens(links, own, rest):
    held = own
    for step in range(links.steps - 1):
        held = jnp.concatenate([held, links.to_expert(held, step)], axis=0)
    last = links.to_expert(held, links.steps - 1)
    other = links.to_core(held[own.shape[0] :])
    first = jnp.concatenate([held, rest, other], axis=0)
    return first, jnp.concatenate([last, links.to_core(last)], axis=0)


def gather_cotangent(links, own, rest):
    half = own.shape[0]
    quarter = half // 2
    held = own[:quarter]
    for step in range(links.steps):
        held = jnp.concatenate([held, links.to_expert(held, step)], axis=0)
    beside = links.to_shard(held[quarter:], 1)
    blocks = links.groups - 1
    both = jnp.stack(
        [held[quarter:].reshape(blocks, quarter, -1), beside.reshape(blocks, quarter, -1)], axis=1
    ).reshape(blocks * half, -1)
    other = links.to_core(both)
    middle = (links.groups // 2 - 1) * half
    first = jnp.concatenate([own, both[:middle], rest, other[:middle]], axis=0)
    return first, jnp.concatenate([both[middle:], other[middle:]], axis=0)


class Sum:
    def __init__(self, links):
        self.links = links

    def second(self, terms):
        self.late, self.sent = terms[0], self.links.to_core(terms[1])

    def first(self, terms):
        self.early, self.early_sent = terms[0], self.links.to_core(terms[1])

    def join_second(self, *after):
        self.late = add(self.late, hold(self.sent, *after))
        self.came = self.links.to_expert(self.late, self.links.steps - 1)
        return self.late

    def join_first(self, *after):
        came = hold(self.came, *after)
        total = self.early.astype(F32) + self.early_sent.astype(F32) + came.astype(F32)
        held = total.astype(BF)
        for step in reversed(range(1, self.links.steps - 1)):
            count = held.shape[0] // 2
            held = add(held[:count], self.links.to_expert(held[count:], step))
        count = held.shape[0] // 2
        self.held = held[:count]
        self.came = self.links.to_expert(held[count:], 0)
        return held

    def join_expert(self, *after):
        held = add(self.held, hold(self.came, *after))
        quarter = held.shape[0] // 2
        self.mine = held[:quarter]
        self.came = self.links.to_shard(held[quarter:], 1)
        return held

    def join_near(self, *after):
        self.mine = add(self.mine, hold(self.came, *after))
        self.came = self.links.to_shard(self.mine, 2)
        return self.mine

    def join_far(self, *after):
        self.mine = add(self.mine, hold(self.came, *after))
        for bit in range(3, log2(self.links.shards)):
            self.mine = add(self.mine, self.links.to_shard(self.mine, bit))
        self.came = self.links.to_shard(self.mine, 1)
        return self.mine

    def join_half(self, *after):
        beside = hold(self.came, *after)
        self.part = jnp.where(
            self.links.deep == 0,
            jnp.concatenate([self.mine, beside], axis=0),
            jnp.concatenate([beside, self.mine], axis=0),
        )
        self.came = self.links.to_core(self.part)
        return self.part

    def rows(self, columns, *after):
        part, other = self.part[:, columns], hold(self.came, *after)[:, columns]
        return jnp.where(
            self.links.core == 0,
            jnp.concatenate([part, other], axis=0),
            jnp.concatenate([other, part], axis=0),
        )


def whole(array):
    return pl.BlockSpec(array.shape, lambda j: (0,) * array.ndim)


def call(kernel, tiles, operands, specs, outs, out_specs, scratch, after, flops, vmem):
    size = sum(a.size * a.dtype.itemsize for a in operands)
    size += sum(a.size * a.dtype.itemsize for a in outs)
    count = len(operands)

    def body(*refs):
        kernel(*refs[:count], *refs[count + len(after) :])

    return pl.pallas_call(
        body,
        grid=(tiles,),
        in_specs=list(specs) + [pl.BlockSpec(memory_space=pl.ANY)] * len(after),
        out_specs=out_specs,
        out_shape=outs,
        scratch_shapes=scratch,
        compiler_params=pltpu.CompilerParams(vmem_limit_bytes=vmem << 20),
        cost_estimate=pl.CostEstimate(flops=flops, bytes_accessed=size, transcendentals=0),
    )(*operands, *after)


def dot(left, right, left_dim, right_dim):
    return lax.dot_general(
        left, right, (((left_dim,), (right_dim,)), ((), ())), preferred_element_type=F32
    )


def front(rows, gate, up, weight):
    pre_gate = dot(rows, gate, 1, 0)
    pre_up = dot(rows, up, 1, 0)
    sigma = jax.nn.sigmoid(pre_gate)
    silu = pre_gate * sigma
    scaled = (weight * (silu * pre_up)).astype(BF)
    slope = (weight * (pre_up * sigma * (1.0 + pre_gate * (1.0 - sigma)))).astype(BF)
    return lax.optimization_barrier(
        (scaled, slope, (weight * silu).astype(BF), pre_up.astype(BF))
    )


def hidden_grads(rows, down, slope, silu):
    raw = dot(rows, down, 1, 1)
    return lax.optimization_barrier(
        ((raw * slope.astype(F32)).astype(BF), (raw * silu.astype(F32)).astype(BF))
    )


def out_terms(scaled, down):
    middle = scaled.shape[0] // 2
    term = dot(scaled, down, 1, 0).astype(BF)
    return term[:middle], term[middle:]


def back_terms(grad_gate, grad_up, pre_up, gate, up, after=()):
    rows, units, width = grad_gate.shape[0], gate.shape[1], gate.shape[0]
    tile = tile_of(width, 512)
    tiles = width // tile
    middle = rows // 2
    nt = (((1,), (1,)), ((), ()))

    def kernel(gate_grad, up_grad, pre_ref, gate_ref, up_ref, keep_ref, send_ref):
        j = pl.program_id(0)
        term = lax.dot_general(gate_grad[...], gate_ref[...], nt, preferred_element_type=F32)
        term += lax.dot_general(up_grad[...], up_ref[...], nt, preferred_element_type=F32)
        term = term.astype(BF)
        columns = pl.ds(pl.multiple_of(j * tile, LANES), tile)
        keep_ref[:, columns] = term[:middle]
        send_ref[:, columns] = term[middle:]

        @pl.when(j == tiles - 1)
        def _():
            lane = lax.broadcasted_iota(jnp.int32, (rows, LANES), 1)
            prob = jnp.sum(
                up_grad[...].astype(F32) * pre_ref[...].astype(F32), axis=1, keepdims=True
            )
            own = jnp.where(lane == lax.axis_index("expert"), prob, 0.0).astype(BF)
            keep_ref[:, width:] = own[:middle]
            send_ref[:, width:] = own[middle:]

    block = pl.BlockSpec((middle, width + LANES), lambda j: (0, 0))
    row = pl.BlockSpec((tile, units), lambda j: (j, 0))
    return call(
        kernel,
        tiles,
        [grad_gate, grad_up, pre_up, gate, up],
        [whole(grad_gate), whole(grad_up), whole(pre_up), row, row],
        [jax.ShapeDtypeStruct((middle, width + LANES), BF)] * 2,
        [block, block],
        [],
        after,
        4 * rows * width * units,
        32,
    )


def per_device(tokens, assignment, route_weight, cotangent, w_gate, w_up, w_down):
    links = Links()
    width = tokens.shape[1]
    gate, up, down = w_gate[0], w_up[0], w_down[0]

    c_own, c_rest = lax.optimization_barrier(tuple(halves(links, cotangent)))
    x_own, x_rest = lax.optimization_barrier(tuple(halves(links, hold(tokens, c_own))))
    received = []
    for offset in range(links.groups):
        there = links.expert ^ offset
        column = jnp.sum(
            jnp.where(hold(assignment, x_own) == there, route_weight, 0.0), axis=1
        )
        received.append(column if offset == 0 else links.to_offset(column, offset))
    weight1, weight2 = order_rows(links, jnp.stack(received))
    x1, x2 = gather_tokens(links, x_own, x_rest)
    c1, c2 = gather_cotangent(links, c_own, c_rest)

    outs, backs = Sum(links), Sum(links)
    scaled1, slope1, silu1, up1 = front(x1, gate, up, weight1)
    scaled2, slope2, silu2, up2 = front(hold(x2, scaled1), gate, up, weight2)
    outs.second(lax.optimization_barrier(out_terms(scaled2, down)))
    gate_grad2, up_grad2 = hidden_grads(hold(c2, outs.late), down, slope2, silu2)
    o_late = outs.join_second(gate_grad2)
    back2 = back_terms(gate_grad2, up_grad2, up2, gate, up, after=[o_late])
    backs.second(back2)
    out1 = lax.optimization_barrier(out_terms(hold(scaled1, *back2), down))
    outs.first(out1)
    b_late = backs.join_second(*out1)
    gate_grad1, up_grad1 = hidden_grads(hold(c1, b_late), down, slope1, silu1)
    o_held = outs.join_first(gate_grad1)
    back1 = back_terms(gate_grad1, up_grad1, up1, gate, up, after=[o_held])
    backs.first(back1)
    o_sum = outs.join_expert(*back1)

    x_all = jnp.concatenate([x1, x2], axis=0)
    c_all = jnp.concatenate([c1, c2], axis=0)
    scaled = jnp.concatenate([scaled1, scaled2], axis=0)
    gate_grad = jnp.concatenate([gate_grad1, gate_grad2], axis=0)
    up_grad = jnp.concatenate([up_grad1, up_grad2], axis=0)
    grad_down = dot(hold(scaled, o_sum), c_all, 0, 0).astype(BF)
    b_held = backs.join_first(grad_down)
    o_near = outs.join_near(b_held)
    grad_gate = dot(hold(x_all, o_near), gate_grad, 0, 0).astype(BF)
    b_sum = backs.join_expert(grad_gate)
    o_far = outs.join_far(b_sum)
    b_near = backs.join_near(o_far)
    grad_up = dot(hold(x_all, b_near), up_grad, 0, 0).astype(BF)
    o_part = outs.join_half(grad_up)
    b_far = backs.join_far(o_part)
    moe_out = outs.rows(slice(0, width), b_far)
    backs.join_half(moe_out)

    grad_tokens = backs.rows(slice(0, width))
    prob_all = backs.rows(slice(width, None)).astype(F32)
    lane = lax.broadcasted_iota(jnp.int32, (1, LANES), 1)
    grad_prob = jnp.stack(
        [
            jnp.sum(jnp.where(lane == assignment[:, k : k + 1], prob_all, 0.0), axis=1)
            for k in range(assignment.shape[1])
        ],
        axis=1,
    )
    grad_prob = grad_prob / route_weight
    return (moe_out, grad_tokens, grad_prob, grad_gate[None], grad_up[None], grad_down[None])


def solution(mesh):
    return jax.shard_map(
        per_device,
        mesh=mesh,
        in_specs=(
            P("expert", None),
            P("expert", None),
            P("expert", None),
            P("expert", None),
            P("expert", None, "fsdp"),
            P("expert", None, "fsdp"),
            P("expert", "fsdp", None),
        ),
        out_specs=(
            P("expert", None),
            P("expert", None),
            P("expert", None),
            P("expert", None, "fsdp"),
            P("expert", None, "fsdp"),
            P("expert", "fsdp", None),
        ),
        check_vma=False,
    )
```

```python
import jax
import jax.numpy as jnp
from jax import lax
from jax.experimental import pallas as pl
from jax.experimental.pallas import tpu as pltpu
from jax.sharding import PartitionSpec as P

AXES = ("expert", "fsdp")
LANES = 128
BACK_VMEM = 32
EARLY_FLOPS = 60_000_000_000
BF = jnp.bfloat16
F32 = jnp.float32


def log2(size):
    return size.bit_length() - 1


def tile_of(size, most):
    tile = most
    while size % tile:
        tile -= LANES
    return tile


def swap(value, groups, shards, partner):
    pairs = []
    for e in range(groups):
        for f in range(shards):
            to_e, to_f = partner(e, f)
            pairs.append((e * shards + f, to_e * shards + to_f))
    return lax.ppermute(value, AXES, pairs)


class Links:
    def __init__(self):
        self.groups = lax.axis_size("expert")
        self.shards = lax.axis_size("fsdp")
        self.steps = log2(self.groups)
        self.expert = lax.axis_index("expert")
        fsdp = lax.axis_index("fsdp")
        self.core = fsdp % 2
        self.deep = (fsdp // 2) % 2

    def order(self, core):
        return [(k + core) % self.steps for k in range(self.steps)]

    def offsets(self, core):
        found = [0]
        for bit in self.order(core):
            found = found + [o ^ (1 << bit) for o in found]
        return found

    def to_core(self, value):
        return swap(value, self.groups, self.shards, lambda e, f: (e, f ^ 1))

    def to_expert(self, value, step):
        orders = [self.order(0), self.order(1)]
        return swap(
            value, self.groups, self.shards, lambda e, f: (e ^ (1 << orders[f % 2][step]), f)
        )

    def to_offset(self, value, offset):
        return swap(value, self.groups, self.shards, lambda e, f: (e ^ offset, f))

    def to_shard(self, value, bit):
        return swap(value, self.groups, self.shards, lambda e, f: (e, f ^ (1 << bit)))


def add(left, right):
    return (left.astype(F32) + right.astype(F32)).astype(BF)


def hold(value, *others):
    return lax.optimization_barrier((value, *others))[0]


def halves(links, rows, routes=(), weight=0):
    count, width = rows.shape
    quarter, groups = count // 4, links.groups
    extra = LANES if routes else 0
    top = routes[0].shape[1] if routes else 0

    def kernel(*refs):
        inputs, (own_ref, rest_ref) = refs[: 1 + len(routes)], refs[1 + len(routes) :][:2]
        names_ref, weights_ref, sems = refs[-3:]
        fsdp = lax.axis_index("fsdp")
        core, deep = fsdp % 2, (fsdp // 2) % 2
        copies = []
        for source, target in zip(inputs[1:], (names_ref, weights_ref)):
            copies.append((source, target))
        for target, side in ((own_ref, core), (rest_ref, 1 - core)):
            for place, part in enumerate((deep, 1 - deep)):
                start = pl.multiple_of((2 * side + part) * quarter, quarter)
                here = pl.ds(place * quarter, quarter)
                copies.append(
                    (inputs[0].at[pl.ds(start, quarter), :], target.at[here, pl.ds(0, width)])
                )
        copies = [
            pltpu.make_async_copy(source, target, sems.at[k])
            for k, (source, target) in enumerate(copies)
        ]
        for copy in copies:
            copy.start()
        for copy in copies:
            copy.wait()
        if routes:
            source = lax.broadcasted_iota(jnp.int32, (count, count), 1)
            index = lax.broadcasted_iota(jnp.int32, (count, count), 0)
            lane = lax.broadcasted_iota(jnp.int32, (1, LANES), 1)
            for target, side in ((own_ref, core), (rest_ref, 1 - core)):
                place = (index // quarter) % 2
                part = jnp.where(place == 0, deep, 1 - deep)
                wanted = (2 * side + part) * quarter + index % quarter
                left = jnp.zeros((count, LANES), F32)
                for k in range(top):
                    chosen = source == wanted
                    names = jnp.where(chosen, names_ref[k : k + 1, :].astype(F32), 0.0)
                    weights = jnp.where(chosen, weights_ref[k : k + 1, :], 0.0)
                    name = jnp.sum(names, axis=1, keepdims=True)
                    weight = jnp.sum(weights, axis=1, keepdims=True)
                    left += jnp.where(name == (lane % groups).astype(F32), weight, 0.0)
                columns = jnp.zeros_like(left)
                for limb in range(3):
                    high = left.astype(BF).astype(F32)
                    columns = jnp.where(lane // groups == limb, high, columns)
                    left = left - high
                target[:, width:] = columns[: 2 * quarter].astype(BF)

    operands = [rows, *(route.T for route in routes)]
    return pl.pallas_call(
        kernel,
        in_specs=[pl.BlockSpec(memory_space=pltpu.HBM)] * len(operands),
        out_specs=[pl.BlockSpec(memory_space=pltpu.VMEM)] * 2,
        out_shape=[jax.ShapeDtypeStruct((2 * quarter, width + extra), BF)] * 2,
        scratch_shapes=[
            pltpu.VMEM((max(top, 1), count), jnp.int32),
            pltpu.VMEM((max(top, 1), count), F32),
            pltpu.SemaphoreType.DMA((6,)),
        ],
        compiler_params=pltpu.CompilerParams(vmem_limit_bytes=(16 if weight else 63) << 20),
        cost_estimate=pl.CostEstimate(flops=weight, bytes_accessed=0, transcendentals=0),
    )(*operands)


class Rows:
    def __init__(self, links, rows, routes=(), weight=0):
        self.links = links
        self.own, self.rest = halves(links, rows, routes, weight)
        self.came = None
        if links.steps > 1:
            self.came = links.to_expert(self.own, 0)

    def send(self, *after):
        links, held, pieces = self.links, self.own, []
        for step in range(links.steps - 1):
            came = hold(self.came, *after) if step == 0 else links.to_expert(held, step)
            held = jnp.concatenate([held, came], axis=0)
            pieces.append(came)
        self.held = held
        self.last = links.to_expert(self.held, links.steps - 1)
        self.other = links.to_core(jnp.concatenate(pieces, axis=0))

    def first(self, *after):
        return jnp.concatenate([self.held, self.rest, hold(self.other, *after)], axis=0)

    def second(self, *after):
        last = hold(self.last, *after)
        return jnp.concatenate([last, self.links.to_core(last)], axis=0)


def joined(pieces, *after):
    return jnp.concatenate(lax.optimization_barrier((*pieces, *after))[: len(pieces)], axis=0)


class Sum:
    def __init__(self, links):
        self.links = links

    def second(self, terms):
        self.late, self.sent = terms[0], self.links.to_core(terms[1])

    def first(self, terms):
        self.early, self.early_sent = terms[0], self.links.to_core(terms[1])

    def join_second(self, *after):
        self.late = add(self.late, hold(self.sent, *after))
        self.came = self.links.to_expert(self.late, self.links.steps - 1)
        return self.late

    def join_first(self, *after):
        came = hold(self.came, *after)
        total = self.early.astype(F32) + self.early_sent.astype(F32) + came.astype(F32)
        held = total.astype(BF)
        for step in reversed(range(1, self.links.steps - 1)):
            count = held.shape[0] // 2
            held = add(held[:count], self.links.to_expert(held[count:], step))
        count = held.shape[0] // 2
        self.held = held[:count]
        self.came = self.links.to_expert(held[count:], 0)
        return held

    def join_expert(self, *after):
        held = add(self.held, hold(self.came, *after))
        quarter = held.shape[0] // 2
        self.mine = held[:quarter]
        self.came = self.links.to_shard(held[quarter:], 1)
        return held

    def join_near(self, *after):
        self.mine = add(self.mine, hold(self.came, *after))
        self.came = self.links.to_shard(self.mine, 2)
        return self.mine

    def join_far(self, *after):
        self.mine = add(self.mine, hold(self.came, *after))
        for bit in range(3, log2(self.links.shards)):
            self.mine = add(self.mine, self.links.to_shard(self.mine, bit))
        self.came = self.links.to_shard(self.mine, 1)
        return self.mine

    def join_half(self, *after):
        beside = hold(self.came, *after)
        self.part = jnp.where(
            self.links.deep == 0,
            jnp.concatenate([self.mine, beside], axis=0),
            jnp.concatenate([beside, self.mine], axis=0),
        )
        self.came = self.links.to_core(self.part)
        return self.part

    def rows(self, columns, *after):
        part, other = self.part[:, columns], hold(self.came, *after)[:, columns]
        return jnp.where(
            self.links.core == 0,
            jnp.concatenate([part, other], axis=0),
            jnp.concatenate([other, part], axis=0),
        )


def dot(left, right, left_dim, right_dim):
    return lax.dot_general(
        left, right, (((left_dim,), (right_dim,)), ((), ())), preferred_element_type=F32
    )


def front(rows, gate, up, *after):
    pre_gate = dot(rows, gate, 1, 0)
    pre_up = dot(hold(rows, pre_gate, *after), up, 1, 0)
    sigma = jax.nn.sigmoid(pre_gate)
    silu = pre_gate * sigma
    hidden = (silu * pre_up).astype(BF)
    slope = (pre_up * sigma * (1.0 + pre_gate * (1.0 - sigma))).astype(BF)
    return lax.optimization_barrier((hidden, slope, silu.astype(BF), pre_up.astype(BF)))


def hidden_grads(rows, down, slope, silu, weight):
    raw = dot(rows, down, 1, 1) * weight
    return lax.optimization_barrier(
        ((raw * slope.astype(F32)).astype(BF), (raw * silu.astype(F32)).astype(BF))
    )


def out_terms(hidden, down, weight):
    middle = hidden.shape[0] // 2
    term = (dot(hidden, down, 1, 0) * weight).astype(BF)
    return term[:middle], term[middle:]


def back_terms(grads_gate, grads_up, pre_ups, gate, up):
    rows, units, width = grads_gate[0].shape[0], gate.shape[1], gate.shape[0]
    chunks = len(grads_gate)
    tile = tile_of(width, 512)
    tiles = width // tile
    middle = rows // 2
    nt = (((1,), (1,)), ((), ()))

    def kernel(*refs):
        grad_refs = refs[: 3 * chunks]
        gate_ref, up_ref = refs[3 * chunks : 3 * chunks + 2]
        outs = refs[3 * chunks + 2 : 3 * chunks + 2 + 2 * chunks]
        gate_all, up_all = refs[-2:]
        j = pl.program_id(0)

        @pl.when(j == 0)
        def _():
            for k in range(chunks):
                gate_all[k * rows : (k + 1) * rows, :] = grad_refs[k][...]
                up_all[k * rows : (k + 1) * rows, :] = grad_refs[chunks + k][...]

        term = lax.dot_general(gate_all[...], gate_ref[...], nt, preferred_element_type=F32)
        term += lax.dot_general(up_all[...], up_ref[...], nt, preferred_element_type=F32)
        term = term.astype(BF)
        columns = pl.ds(pl.multiple_of(j * tile, LANES), tile)
        for k in range(2 * chunks):
            outs[k][:, columns] = term[k * middle : (k + 1) * middle]

        @pl.when(j == tiles - 1)
        def _():
            lane = lax.broadcasted_iota(jnp.int32, (rows, LANES), 1)
            for k in range(chunks):
                prob = jnp.sum(
                    grad_refs[chunks + k][...].astype(F32)
                    * grad_refs[2 * chunks + k][...].astype(F32),
                    axis=1,
                    keepdims=True,
                )
                own = jnp.where(lane == lax.axis_index("expert"), prob, 0.0).astype(BF)
                outs[2 * k][:, width:] = own[:middle]
                outs[2 * k + 1][:, width:] = own[middle:]

    operands = [*grads_gate, *grads_up, *pre_ups, gate, up]
    size = sum(a.size * a.dtype.itemsize for a in operands)
    size += 2 * chunks * middle * (width + LANES) * 2
    block = pl.BlockSpec((middle, width + LANES), lambda j: (0, 0))
    full = pl.BlockSpec((rows, units), lambda j: (0, 0))
    row = pl.BlockSpec((tile, units), lambda j: (j, 0))
    outs = pl.pallas_call(
        kernel,
        grid=(tiles,),
        in_specs=[full] * (3 * chunks) + [row] * 2,
        out_specs=[block] * (2 * chunks),
        out_shape=[jax.ShapeDtypeStruct((middle, width + LANES), BF)] * (2 * chunks),
        scratch_shapes=[pltpu.VMEM((chunks * rows, units), BF)] * 2,
        compiler_params=pltpu.CompilerParams(vmem_limit_bytes=BACK_VMEM << 20),
        cost_estimate=pl.CostEstimate(
            flops=0, bytes_accessed=0, transcendentals=0
        ),
    )(*operands)
    return [(outs[2 * k], outs[2 * k + 1]) for k in range(chunks)]


def per_device(tokens, assignment, route_weight, cotangent, w_gate, w_up, w_down):
    links = Links()
    width = tokens.shape[1]
    gate, up, down = w_gate[0], w_up[0], w_down[0]
    lane = lax.broadcasted_iota(jnp.int32, (1, LANES), 1)

    x = Rows(links, tokens, (assignment, route_weight))
    c = Rows(links, hold(cotangent, x.own), weight=EARLY_FLOPS)

    def weights(chunk):
        own = jnp.logical_and(lane % links.groups == links.expert, lane < 3 * links.groups)
        limbs = jnp.where(own, chunk[:, width:].astype(F32), 0.0)
        return jnp.sum(limbs, axis=1, keepdims=True)

    outs, backs = Sum(links), Sum(links)
    x.send()
    x1 = x.first()
    hidden1, slope1, silu1, up1 = front(x1[:, :width], gate, up, c.came)
    weight1 = weights(x1)
    c.send(x1)
    c1 = c.first()
    gate_grad1, up_grad1 = hidden_grads(c1, down, slope1, silu1, weight1)
    x2 = x.second()
    x2 = hold(x2, gate_grad1)
    hidden2, slope2, silu2, up2 = front(x2[:, :width], gate, up)
    weight2 = weights(x2)
    out2 = lax.optimization_barrier(out_terms(hidden2, down, weight2))
    outs.second(out2)
    out1 = lax.optimization_barrier(out_terms(hold(hidden1, *out2), down, weight1))
    outs.first(out1)
    o_late = outs.join_second(*out1)
    c2 = c.second(hidden2)
    gate_grad2, up_grad2 = hidden_grads(hold(c2, o_late), down, slope2, silu2, weight2)
    (back2,) = back_terms([gate_grad2], [up_grad2], [up2], gate, up)
    backs.second(back2)
    o_held = outs.join_first(*back2)
    (back1,) = back_terms([hold(gate_grad1, o_held)], [up_grad1], [up1], gate, up)
    backs.first(back1)
    b_late = backs.join_second(*back1)

    weight = jnp.concatenate([weight1, weight2], axis=0)
    scaled = (joined([hidden1, hidden2], b_late).astype(F32) * weight).astype(BF)
    grad_down = dot(scaled, joined([c1, c2], b_late), 0, 0).astype(BF)
    o_sum = outs.join_expert(grad_down)
    b_held = backs.join_first(o_sum)
    x_all = joined([x1, x2], b_held)[:, :width]
    grad_gate = dot(x_all, joined([gate_grad1, gate_grad2]), 0, 0).astype(BF)
    b_sum = backs.join_expert(grad_gate)
    o_near = outs.join_near(b_sum)
    b_near = backs.join_near(o_near)
    grad_up = dot(hold(x_all, b_near), joined([up_grad1, up_grad2]), 0, 0).astype(BF)
    o_far = outs.join_far(grad_up)
    b_far = backs.join_far(o_far)
    o_part = outs.join_half(b_far)
    backs.join_half(o_part)
    moe_out = outs.rows(slice(0, width), backs.part)

    grad_tokens = backs.rows(slice(0, width))
    prob_all = backs.rows(slice(width, None)).astype(F32)
    grad_prob = jnp.stack(
        [
            jnp.sum(jnp.where(lane == assignment[:, k : k + 1], prob_all, 0.0), axis=1)
            for k in range(assignment.shape[1])
        ],
        axis=1,
    )
    grad_prob = grad_prob / route_weight
    return (moe_out, grad_tokens, grad_prob, grad_gate[None], grad_up[None], grad_down[None])


def solution(mesh):
    return jax.shard_map(
        per_device,
        mesh=mesh,
        in_specs=(
            P("expert", None),
            P("expert", None),
            P("expert", None),
            P("expert", None),
            P("expert", None, "fsdp"),
            P("expert", None, "fsdp"),
            P("expert", "fsdp", None),
        ),
        out_specs=(
            P("expert", None),
            P("expert", None),
            P("expert", None),
            P("expert", None, "fsdp"),
            P("expert", None, "fsdp"),
            P("expert", "fsdp", None),
        ),
        check_vma=False,
    )
```

```python
import jax
import jax.numpy as jnp
from jax import lax
from jax.experimental import pallas as pl
from jax.experimental.pallas import tpu as pltpu
from jax.sharding import PartitionSpec as P

AXES = ("expert", "fsdp")
LANES = 128
BACK_VMEM = 32
EARLY_FLOPS = 60_000_000_000
BF = jnp.bfloat16
F32 = jnp.float32


def log2(size):
    return size.bit_length() - 1


def tile_of(size, most):
    tile = most
    while size % tile:
        tile -= LANES
    return tile


def swap(value, groups, shards, partner):
    pairs = []
    for e in range(groups):
        for f in range(shards):
            to_e, to_f = partner(e, f)
            pairs.append((e * shards + f, to_e * shards + to_f))
    return lax.ppermute(value, AXES, pairs)


class Links:
    def __init__(self):
        self.groups = lax.axis_size("expert")
        self.shards = lax.axis_size("fsdp")
        self.steps = log2(self.groups)
        self.expert = lax.axis_index("expert")
        fsdp = lax.axis_index("fsdp")
        self.core = fsdp % 2
        self.deep = (fsdp // 2) % 2

    def order(self, core):
        return [(k + core) % self.steps for k in range(self.steps)]

    def offsets(self, core):
        found = [0]
        for bit in self.order(core):
            found = found + [o ^ (1 << bit) for o in found]
        return found

    def to_core(self, value):
        return swap(value, self.groups, self.shards, lambda e, f: (e, f ^ 1))

    def to_expert(self, value, step):
        orders = [self.order(0), self.order(1)]
        return swap(
            value, self.groups, self.shards, lambda e, f: (e ^ (1 << orders[f % 2][step]), f)
        )

    def to_offset(self, value, offset):
        return swap(value, self.groups, self.shards, lambda e, f: (e ^ offset, f))

    def to_shard(self, value, bit):
        return swap(value, self.groups, self.shards, lambda e, f: (e, f ^ (1 << bit)))


def add(left, right):
    return (left.astype(F32) + right.astype(F32)).astype(BF)


def hold(value, *others):
    return lax.optimization_barrier((value, *others))[0]


def halves(links, rows, routes=(), weight=0):
    count, width = rows.shape
    quarter, groups = count // 4, links.groups
    extra = LANES if routes else 0
    top = routes[0].shape[1] if routes else 0

    def kernel(*refs):
        inputs, (own_ref, rest_ref) = refs[: 1 + len(routes)], refs[1 + len(routes) :][:2]
        names_ref, weights_ref, sems = refs[-3:]
        fsdp = lax.axis_index("fsdp")
        core, deep = fsdp % 2, (fsdp // 2) % 2
        copies = []
        for source, target in zip(inputs[1:], (names_ref, weights_ref)):
            copies.append((source, target))
        for target, side in ((own_ref, core), (rest_ref, 1 - core)):
            for place, part in enumerate((deep, 1 - deep)):
                start = pl.multiple_of((2 * side + part) * quarter, quarter)
                here = pl.ds(place * quarter, quarter)
                copies.append(
                    (inputs[0].at[pl.ds(start, quarter), :], target.at[here, pl.ds(0, width)])
                )
        copies = [
            pltpu.make_async_copy(source, target, sems.at[k])
            for k, (source, target) in enumerate(copies)
        ]
        for copy in copies:
            copy.start()
        for copy in copies:
            copy.wait()
        if routes:
            source = lax.broadcasted_iota(jnp.int32, (count, count), 1)
            index = lax.broadcasted_iota(jnp.int32, (count, count), 0)
            lane = lax.broadcasted_iota(jnp.int32, (1, LANES), 1)
            for target, side in ((own_ref, core), (rest_ref, 1 - core)):
                place = (index // quarter) % 2
                part = jnp.where(place == 0, deep, 1 - deep)
                wanted = (2 * side + part) * quarter + index % quarter
                left = jnp.zeros((count, LANES), F32)
                for k in range(top):
                    chosen = source == wanted
                    names = jnp.where(chosen, names_ref[k : k + 1, :].astype(F32), 0.0)
                    weights = jnp.where(chosen, weights_ref[k : k + 1, :], 0.0)
                    name = jnp.sum(names, axis=1, keepdims=True)
                    weight = jnp.sum(weights, axis=1, keepdims=True)
                    left += jnp.where(name == (lane % groups).astype(F32), weight, 0.0)
                columns = jnp.zeros_like(left)
                for limb in range(3):
                    high = left.astype(BF).astype(F32)
                    columns = jnp.where(lane // groups == limb, high, columns)
                    left = left - high
                target[:, width:] = columns[: 2 * quarter].astype(BF)

    operands = [rows, *(route.T for route in routes)]
    return pl.pallas_call(
        kernel,
        in_specs=[pl.BlockSpec(memory_space=pltpu.HBM)] * len(operands),
        out_specs=[pl.BlockSpec(memory_space=pltpu.VMEM)] * 2,
        out_shape=[jax.ShapeDtypeStruct((2 * quarter, width + extra), BF)] * 2,
        scratch_shapes=[
            pltpu.VMEM((max(top, 1), count), jnp.int32),
            pltpu.VMEM((max(top, 1), count), F32),
            pltpu.SemaphoreType.DMA((6,)),
        ],
        compiler_params=pltpu.CompilerParams(vmem_limit_bytes=(16 if weight else 63) << 20),
        cost_estimate=pl.CostEstimate(flops=weight, bytes_accessed=0, transcendentals=0),
    )(*operands)


class Rows:
    def __init__(self, links, rows, routes=(), weight=0):
        self.links = links
        self.own, self.rest = halves(links, rows, routes, weight)
        self.came = None
        if links.steps > 1:
            self.came = links.to_expert(self.own, 0)

    def send(self, *after):
        links, held, pieces = self.links, self.own, []
        for step in range(links.steps - 1):
            came = hold(self.came, *after) if step == 0 else links.to_expert(held, step)
            held = jnp.concatenate([held, came], axis=0)
            pieces.append(came)
        self.held = held
        self.last = links.to_expert(self.held, links.steps - 1)
        self.other = links.to_core(jnp.concatenate(pieces, axis=0))

    def first(self, *after):
        return jnp.concatenate([self.held, self.rest, hold(self.other, *after)], axis=0)

    def second(self, *after):
        last = hold(self.last, *after)
        return jnp.concatenate([last, self.links.to_core(last)], axis=0)


def joined(pieces, *after):
    return jnp.concatenate(lax.optimization_barrier((*pieces, *after))[: len(pieces)], axis=0)


class Sum:
    def __init__(self, links):
        self.links = links

    def second(self, terms):
        self.late, self.sent = terms[0], self.links.to_core(terms[1])

    def first(self, terms):
        self.early, self.early_sent = terms[0], self.links.to_core(terms[1])

    def join_second(self, *after):
        self.late = add(self.late, hold(self.sent, *after))
        self.came = self.links.to_expert(self.late, self.links.steps - 1)
        return self.late

    def join_first(self, *after):
        came = hold(self.came, *after)
        total = self.early.astype(F32) + self.early_sent.astype(F32) + came.astype(F32)
        held = total.astype(BF)
        for step in reversed(range(1, self.links.steps - 1)):
            count = held.shape[0] // 2
            held = add(held[:count], self.links.to_expert(held[count:], step))
        count = held.shape[0] // 2
        self.held = held[:count]
        self.came = self.links.to_expert(held[count:], 0)
        return held

    def join_expert(self, *after):
        held = add(self.held, hold(self.came, *after))
        quarter = held.shape[0] // 2
        self.mine = held[:quarter]
        self.came = self.links.to_shard(held[quarter:], 1)
        return held

    def join_near(self, *after):
        self.mine = add(self.mine, hold(self.came, *after))
        self.came = self.links.to_shard(self.mine, 2)
        return self.mine

    def join_far(self, *after):
        self.mine = add(self.mine, hold(self.came, *after))
        for bit in range(3, log2(self.links.shards)):
            self.mine = add(self.mine, self.links.to_shard(self.mine, bit))
        return self.mine

    def send_half(self, *after):
        self.came = self.links.to_shard(hold(self.mine, *after), 1)

    def join_half(self, *after):
        beside = hold(self.came, *after)
        self.part = jnp.where(
            self.links.deep == 0,
            jnp.concatenate([self.mine, beside], axis=0),
            jnp.concatenate([beside, self.mine], axis=0),
        )
        self.came = self.links.to_core(self.part)
        return self.part

    def rows(self, columns, *after):
        part, other = self.part[:, columns], hold(self.came, *after)[:, columns]
        return jnp.where(
            self.links.core == 0,
            jnp.concatenate([part, other], axis=0),
            jnp.concatenate([other, part], axis=0),
        )


def dot(left, right, left_dim, right_dim):
    return lax.dot_general(
        left, right, (((left_dim,), (right_dim,)), ((), ())), preferred_element_type=F32
    )


def front(rows, gate, up, *after):
    pre_gate = dot(rows, gate, 1, 0)
    pre_up = dot(hold(rows, pre_gate, *after), up, 1, 0)
    sigma = jax.nn.sigmoid(pre_gate)
    silu = pre_gate * sigma
    hidden = (silu * pre_up).astype(BF)
    slope = (pre_up * sigma * (1.0 + pre_gate * (1.0 - sigma))).astype(BF)
    return lax.optimization_barrier((hidden, slope, silu.astype(BF), pre_up.astype(BF)))


def hidden_grads(rows, down, slope, silu, weight):
    raw = dot(rows, down, 1, 1) * weight
    return lax.optimization_barrier(
        ((raw * slope.astype(F32)).astype(BF), (raw * silu.astype(F32)).astype(BF))
    )


def out_terms(hidden, down, weight):
    middle = hidden.shape[0] // 2
    term = (dot(hidden, down, 1, 0) * weight).astype(BF)
    return term[:middle], term[middle:]


def back_terms(grad_gate, grad_up, pre_up, gate, up):
    rows, units, width = grad_gate.shape[0], gate.shape[1], gate.shape[0]
    tile = tile_of(width, 512)
    tiles = width // tile
    middle = rows // 2
    nt = (((1,), (1,)), ((), ()))

    def kernel(gate_grad, up_grad, pre_ref, gate_ref, up_ref, keep_ref, send_ref):
        j = pl.program_id(0)
        term = lax.dot_general(gate_grad[...], gate_ref[...], nt, preferred_element_type=F32)
        term += lax.dot_general(up_grad[...], up_ref[...], nt, preferred_element_type=F32)
        term = term.astype(BF)
        columns = pl.ds(pl.multiple_of(j * tile, LANES), tile)
        keep_ref[:, columns] = term[:middle]
        send_ref[:, columns] = term[middle:]

        @pl.when(j == tiles - 1)
        def _():
            lane = lax.broadcasted_iota(jnp.int32, (rows, LANES), 1)
            prob = jnp.sum(
                up_grad[...].astype(F32) * pre_ref[...].astype(F32), axis=1, keepdims=True
            )
            own = jnp.where(lane == lax.axis_index("expert"), prob, 0.0).astype(BF)
            keep_ref[:, width:] = own[:middle]
            send_ref[:, width:] = own[middle:]

    block = pl.BlockSpec((middle, width + LANES), lambda j: (0, 0))
    full = pl.BlockSpec((rows, units), lambda j: (0, 0))
    row = pl.BlockSpec((tile, units), lambda j: (j, 0))
    return pl.pallas_call(
        kernel,
        grid=(tiles,),
        in_specs=[full] * 3 + [row] * 2,
        out_specs=[block] * 2,
        out_shape=[jax.ShapeDtypeStruct((middle, width + LANES), BF)] * 2,
        compiler_params=pltpu.CompilerParams(vmem_limit_bytes=BACK_VMEM << 20),
        cost_estimate=pl.CostEstimate(flops=0, bytes_accessed=0, transcendentals=0),
    )(grad_gate, grad_up, pre_up, gate, up)


def per_device(tokens, assignment, route_weight, cotangent, w_gate, w_up, w_down):
    links = Links()
    width = tokens.shape[1]
    gate, up, down = w_gate[0], w_up[0], w_down[0]
    lane = lax.broadcasted_iota(jnp.int32, (1, LANES), 1)

    x = Rows(links, tokens, (assignment, route_weight))
    c = Rows(links, hold(cotangent, x.own), weight=EARLY_FLOPS)

    def weights(chunk):
        own = jnp.logical_and(lane % links.groups == links.expert, lane < 3 * links.groups)
        limbs = jnp.where(own, chunk[:, width:].astype(F32), 0.0)
        return jnp.sum(limbs, axis=1, keepdims=True)

    outs, backs = Sum(links), Sum(links)
    x.send()
    x1 = x.first()
    hidden1, slope1, silu1, up1 = front(x1[:, :width], gate, up, c.came)
    weight1 = weights(x1)
    c.send(x1)
    c1 = c.first()
    gate_grad1, up_grad1 = hidden_grads(c1, down, slope1, silu1, weight1)
    x2 = x.second()
    x2 = hold(x2, gate_grad1)
    hidden2, slope2, silu2, up2 = front(x2[:, :width], gate, up)
    weight2 = weights(x2)
    out2 = lax.optimization_barrier(out_terms(hidden2, down, weight2))
    outs.second(out2)
    out1 = lax.optimization_barrier(out_terms(hold(hidden1, *out2), down, weight1))
    outs.first(out1)
    o_late = outs.join_second(*out1)
    c2 = c.second(hidden2)
    gate_grad2, up_grad2 = hidden_grads(hold(c2, o_late), down, slope2, silu2, weight2)
    back2 = back_terms(gate_grad2, up_grad2, up2, gate, up)
    backs.second(back2)
    o_held = outs.join_first(*back2)
    back1 = back_terms(hold(gate_grad1, o_held), up_grad1, up1, gate, up)
    backs.first(back1)
    b_late = backs.join_second(*back1)
    weight = jnp.concatenate([weight1, weight2], axis=0)
    o_sum = outs.join_expert(b_late)
    scaled = (joined([hidden1, hidden2], o_sum).astype(F32) * weight).astype(BF)
    grad_down = dot(scaled, joined([c1, c2], o_sum), 0, 0).astype(BF)
    o_near = outs.join_near(grad_down)
    b_held = backs.join_first(o_near)
    x_all = joined([x1, x2], b_held)[:, :width]
    grad_gate = dot(x_all, joined([gate_grad1, gate_grad2]), 0, 0).astype(BF)
    b_sum = backs.join_expert(grad_gate)
    o_far = outs.join_far(b_sum)
    b_near = backs.join_near(o_far)
    outs.send_half(b_near)
    grad_up = dot(hold(x_all, b_near), joined([up_grad1, up_grad2]), 0, 0).astype(BF)
    b_far = backs.join_far(grad_up)
    backs.send_half()
    o_part = outs.join_half(b_far)
    backs.join_half(o_part)
    moe_out = outs.rows(slice(0, width), backs.part)

    grad_tokens = backs.rows(slice(0, width))
    prob_all = backs.rows(slice(width, None)).astype(F32)
    grad_prob = jnp.stack(
        [
            jnp.sum(jnp.where(lane == assignment[:, k : k + 1], prob_all, 0.0), axis=1)
            for k in range(assignment.shape[1])
        ],
        axis=1,
    )
    grad_prob = grad_prob / route_weight
    return (moe_out, grad_tokens, grad_prob, grad_gate[None], grad_up[None], grad_down[None])


def solution(mesh):
    return jax.shard_map(
        per_device,
        mesh=mesh,
        in_specs=(
            P("expert", None),
            P("expert", None),
            P("expert", None),
            P("expert", None),
            P("expert", None, "fsdp"),
            P("expert", None, "fsdp"),
            P("expert", "fsdp", None),
        ),
        out_specs=(
            P("expert", None),
            P("expert", None),
            P("expert", None),
            P("expert", None, "fsdp"),
            P("expert", None, "fsdp"),
            P("expert", "fsdp", None),
        ),
        check_vma=False,
    )
```

```python
import jax
import jax.numpy as jnp
from jax import lax
from jax.experimental import pallas as pl
from jax.experimental.pallas import tpu as pltpu
from jax.sharding import PartitionSpec as P

AXES = ("expert", "fsdp")
LANES = 128
BACK_VMEM = 32
EARLY_FLOPS = 60_000_000_000
BF = jnp.bfloat16
F32 = jnp.float32


def log2(size):
    return size.bit_length() - 1


def tile_of(size, most):
    tile = most
    while size % tile:
        tile -= LANES
    return tile


def swap(value, groups, shards, partner):
    pairs = []
    for e in range(groups):
        for f in range(shards):
            to_e, to_f = partner(e, f)
            pairs.append((e * shards + f, to_e * shards + to_f))
    return lax.ppermute(value, AXES, pairs)


class Links:
    def __init__(self):
        self.groups = lax.axis_size("expert")
        self.shards = lax.axis_size("fsdp")
        self.steps = log2(self.groups)
        self.expert = lax.axis_index("expert")
        fsdp = lax.axis_index("fsdp")
        self.core = fsdp % 2
        self.deep = (fsdp // 2) % 2

    def order(self, core):
        return [(k + core) % self.steps for k in range(self.steps)]

    def offsets(self, core):
        found = [0]
        for bit in self.order(core):
            found = found + [o ^ (1 << bit) for o in found]
        return found

    def to_core(self, value):
        return swap(value, self.groups, self.shards, lambda e, f: (e, f ^ 1))

    def to_expert(self, value, step):
        orders = [self.order(0), self.order(1)]
        return swap(
            value, self.groups, self.shards, lambda e, f: (e ^ (1 << orders[f % 2][step]), f)
        )

    def to_offset(self, value, offset):
        return swap(value, self.groups, self.shards, lambda e, f: (e ^ offset, f))

    def to_shard(self, value, bit):
        return swap(value, self.groups, self.shards, lambda e, f: (e, f ^ (1 << bit)))


def add(left, right):
    return (left.astype(F32) + right.astype(F32)).astype(BF)


def hold(value, *others):
    return lax.optimization_barrier((value, *others))[0]


def halves(links, rows, routes=(), weight=0):
    count, width = rows.shape
    quarter, groups = count // 4, links.groups
    extra = LANES if routes else 0
    top = routes[0].shape[1] if routes else 0

    def kernel(*refs):
        inputs, (own_ref, rest_ref) = refs[: 1 + len(routes)], refs[1 + len(routes) :][:2]
        names_ref, weights_ref, sems = refs[-3:]
        fsdp = lax.axis_index("fsdp")
        core, deep = fsdp % 2, (fsdp // 2) % 2
        copies = []
        for source, target in zip(inputs[1:], (names_ref, weights_ref)):
            copies.append((source, target))
        for target, side in ((own_ref, core), (rest_ref, 1 - core)):
            for place, part in enumerate((deep, 1 - deep)):
                start = pl.multiple_of((2 * side + part) * quarter, quarter)
                here = pl.ds(place * quarter, quarter)
                copies.append(
                    (inputs[0].at[pl.ds(start, quarter), :], target.at[here, pl.ds(0, width)])
                )
        copies = [
            pltpu.make_async_copy(source, target, sems.at[k])
            for k, (source, target) in enumerate(copies)
        ]
        for copy in copies:
            copy.start()
        for copy in copies:
            copy.wait()
        if routes:
            source = lax.broadcasted_iota(jnp.int32, (count, count), 1)
            index = lax.broadcasted_iota(jnp.int32, (count, count), 0)
            lane = lax.broadcasted_iota(jnp.int32, (1, LANES), 1)
            for target, side in ((own_ref, core), (rest_ref, 1 - core)):
                place = (index // quarter) % 2
                part = jnp.where(place == 0, deep, 1 - deep)
                wanted = (2 * side + part) * quarter + index % quarter
                left = jnp.zeros((count, LANES), F32)
                for k in range(top):
                    chosen = source == wanted
                    names = jnp.where(chosen, names_ref[k : k + 1, :].astype(F32), 0.0)
                    weights = jnp.where(chosen, weights_ref[k : k + 1, :], 0.0)
                    name = jnp.sum(names, axis=1, keepdims=True)
                    weight = jnp.sum(weights, axis=1, keepdims=True)
                    left += jnp.where(name == (lane % groups).astype(F32), weight, 0.0)
                columns = jnp.zeros_like(left)
                for limb in range(3):
                    high = left.astype(BF).astype(F32)
                    columns = jnp.where(lane // groups == limb, high, columns)
                    left = left - high
                target[:, width:] = columns[: 2 * quarter].astype(BF)

    operands = [rows, *(route.T for route in routes)]
    return pl.pallas_call(
        kernel,
        in_specs=[pl.BlockSpec(memory_space=pltpu.HBM)] * len(operands),
        out_specs=[pl.BlockSpec(memory_space=pltpu.VMEM)] * 2,
        out_shape=[jax.ShapeDtypeStruct((2 * quarter, width + extra), BF)] * 2,
        scratch_shapes=[
            pltpu.VMEM((max(top, 1), count), jnp.int32),
            pltpu.VMEM((max(top, 1), count), F32),
            pltpu.SemaphoreType.DMA((6,)),
        ],
        compiler_params=pltpu.CompilerParams(vmem_limit_bytes=(16 if weight else 63) << 20),
        cost_estimate=pl.CostEstimate(flops=weight, bytes_accessed=0, transcendentals=0),
    )(*operands)


class Rows:
    def __init__(self, links, rows, routes=(), weight=0):
        self.links = links
        self.own, self.rest = halves(links, rows, routes, weight)
        self.came = None
        if links.steps > 1:
            self.came = links.to_expert(self.own, 0)

    def send(self, *after):
        links, held, pieces = self.links, self.own, []
        for step in range(links.steps - 1):
            came = hold(self.came, *after) if step == 0 else links.to_expert(held, step)
            held = jnp.concatenate([held, came], axis=0)
            pieces.append(came)
        self.held = held
        self.last = links.to_expert(self.held, links.steps - 1)
        self.other = links.to_core(jnp.concatenate(pieces, axis=0))

    def first(self, *after):
        return jnp.concatenate([self.held, self.rest, hold(self.other, *after)], axis=0)

    def second(self, *after):
        last = hold(self.last, *after)
        return jnp.concatenate([last, self.links.to_core(last)], axis=0)


def joined(pieces, *after):
    return jnp.concatenate(lax.optimization_barrier((*pieces, *after))[: len(pieces)], axis=0)


class Sum:
    def __init__(self, links):
        self.links = links

    def second(self, terms):
        self.late, self.sent = terms[0], self.links.to_core(terms[1])

    def first(self, terms):
        self.early, self.early_sent = terms[0], self.links.to_core(terms[1])

    def join_second(self, *after):
        self.late = add(self.late, hold(self.sent, *after))
        self.came = self.links.to_expert(self.late, self.links.steps - 1)
        return self.late

    def join_first(self, *after):
        came = hold(self.came, *after)
        total = self.early.astype(F32) + self.early_sent.astype(F32) + came.astype(F32)
        held = total.astype(BF)
        for step in reversed(range(1, self.links.steps - 1)):
            count = held.shape[0] // 2
            held = add(held[:count], self.links.to_expert(held[count:], step))
        count = held.shape[0] // 2
        self.held = held[:count]
        self.came = self.links.to_expert(held[count:], 0)
        return held

    def join_expert(self, *after):
        held = add(self.held, hold(self.came, *after))
        quarter = held.shape[0] // 2
        self.mine = held[:quarter]
        self.came = self.links.to_shard(held[quarter:], 1)
        return held

    def join_near(self, *after):
        self.mine = add(self.mine, hold(self.came, *after))
        self.came = self.links.to_shard(self.mine, 2)
        return self.mine

    def join_far(self, *after):
        self.mine = add(self.mine, hold(self.came, *after))
        for bit in range(3, log2(self.links.shards)):
            self.mine = add(self.mine, self.links.to_shard(self.mine, bit))
        return self.mine

    def send_half(self, *after):
        self.came = self.links.to_shard(hold(self.mine, *after), 1)

    def join_half(self, *after):
        beside = hold(self.came, *after)
        self.part = jnp.where(
            self.links.deep == 0,
            jnp.concatenate([self.mine, beside], axis=0),
            jnp.concatenate([beside, self.mine], axis=0),
        )
        self.came = self.links.to_core(self.part)
        return self.part

    def rows(self, columns, *after):
        part, other = self.part[:, columns], hold(self.came, *after)[:, columns]
        both = lax.optimization_barrier(jnp.concatenate([part, part], axis=0))
        start = (1 - self.links.core) * part.shape[0]
        return lax.dynamic_update_slice_in_dim(both, other, start, 0)


def dot(left, right, left_dim, right_dim):
    return lax.dot_general(
        left, right, (((left_dim,), (right_dim,)), ((), ())), preferred_element_type=F32
    )


def front(rows, gate, up, *after):
    pre_gate = dot(rows, gate, 1, 0)
    pre_up = dot(hold(rows, pre_gate, *after), up, 1, 0)
    sigma = jax.nn.sigmoid(pre_gate)
    silu = pre_gate * sigma
    hidden = (silu * pre_up).astype(BF)
    slope = (pre_up * sigma * (1.0 + pre_gate * (1.0 - sigma))).astype(BF)
    return lax.optimization_barrier((hidden, slope, silu.astype(BF), pre_up.astype(BF)))


def hidden_grads(rows, down, slope, silu, weight):
    raw = dot(rows, down, 1, 1) * weight
    return lax.optimization_barrier(
        ((raw * slope.astype(F32)).astype(BF), (raw * silu.astype(F32)).astype(BF))
    )


def out_terms(hidden, down, weight):
    middle = hidden.shape[0] // 2
    term = (dot(hidden, down, 1, 0) * weight).astype(BF)
    return term[:middle], term[middle:]


def back_terms(grad_gate, grad_up, pre_up, gate, up):
    rows, units, width = grad_gate.shape[0], gate.shape[1], gate.shape[0]
    tile = tile_of(width, 768)
    tiles = width // tile
    middle = rows // 2
    nt = (((1,), (1,)), ((), ()))

    def kernel(gate_grad, up_grad, pre_ref, gate_ref, up_ref, keep_ref, send_ref):
        j = pl.program_id(0)
        term = lax.dot_general(gate_grad[...], gate_ref[...], nt, preferred_element_type=F32)
        term += lax.dot_general(up_grad[...], up_ref[...], nt, preferred_element_type=F32)
        term = term.astype(BF)
        columns = pl.ds(pl.multiple_of(j * tile, LANES), tile)
        keep_ref[:, columns] = term[:middle]
        send_ref[:, columns] = term[middle:]

        @pl.when(j == tiles - 1)
        def _():
            lane = lax.broadcasted_iota(jnp.int32, (rows, LANES), 1)
            prob = jnp.sum(
                up_grad[...].astype(F32) * pre_ref[...].astype(F32), axis=1, keepdims=True
            )
            own = jnp.where(lane == lax.axis_index("expert"), prob, 0.0).astype(BF)
            keep_ref[:, width:] = own[:middle]
            send_ref[:, width:] = own[middle:]

    block = pl.BlockSpec((middle, width + LANES), lambda j: (0, 0))
    full = pl.BlockSpec((rows, units), lambda j: (0, 0))
    row = pl.BlockSpec((tile, units), lambda j: (j, 0))
    return pl.pallas_call(
        kernel,
        grid=(tiles,),
        in_specs=[full] * 3 + [row] * 2,
        out_specs=[block] * 2,
        out_shape=[jax.ShapeDtypeStruct((middle, width + LANES), BF)] * 2,
        compiler_params=pltpu.CompilerParams(vmem_limit_bytes=24 << 20),
        cost_estimate=pl.CostEstimate(flops=0, bytes_accessed=0, transcendentals=0),
    )(grad_gate, grad_up, pre_up, gate, up)


def per_device(tokens, assignment, route_weight, cotangent, w_gate, w_up, w_down):
    links = Links()
    width = tokens.shape[1]
    gate, up, down = w_gate[0], w_up[0], w_down[0]
    lane = lax.broadcasted_iota(jnp.int32, (1, LANES), 1)

    x = Rows(links, tokens, (assignment, route_weight))
    c = Rows(links, hold(cotangent, x.own), weight=EARLY_FLOPS)

    def weights(chunk):
        own = jnp.logical_and(lane % links.groups == links.expert, lane < 3 * links.groups)
        limbs = jnp.where(own, chunk[:, width:].astype(F32), 0.0)
        return jnp.sum(limbs, axis=1, keepdims=True)

    outs, backs = Sum(links), Sum(links)
    x.send()
    x1 = x.first()
    hidden1, slope1, silu1, up1 = front(x1[:, :width], gate, up, c.came)
    weight1 = weights(x1)
    c.send(x1)
    c1 = c.first()
    gate_grad1, up_grad1 = hidden_grads(c1, down, slope1, silu1, weight1)
    x2 = x.second()
    x2 = hold(x2, gate_grad1)
    hidden2, slope2, silu2, up2 = front(x2[:, :width], gate, up)
    weight2 = weights(x2)
    out2 = lax.optimization_barrier(out_terms(hidden2, down, weight2))
    outs.second(out2)
    out1 = lax.optimization_barrier(out_terms(hold(hidden1, *out2), down, weight1))
    outs.first(out1)
    o_late = outs.join_second(*out1)
    c2 = c.second(hidden2)
    gate_grad2, up_grad2 = hidden_grads(hold(c2, o_late), down, slope2, silu2, weight2)
    back2 = back_terms(gate_grad2, up_grad2, up2, gate, up)
    backs.second(back2)
    o_held = outs.join_first(*back2)
    back1 = back_terms(hold(gate_grad1, o_held), up_grad1, up1, gate, up)
    backs.first(back1)
    b_late = backs.join_second(*back1)
    weight = jnp.concatenate([weight1, weight2], axis=0)
    o_sum = outs.join_expert(b_late)
    scaled = (joined([hidden1, hidden2], o_sum).astype(F32) * weight).astype(BF)
    grad_down = dot(scaled, joined([c1, c2], o_sum), 0, 0).astype(BF)
    o_near = outs.join_near(grad_down)
    b_held = backs.join_first(o_near)
    x_all = joined([x1, x2], b_held)[:, :width]
    grad_gate = dot(x_all, joined([gate_grad1, gate_grad2]), 0, 0).astype(BF)
    b_sum = backs.join_expert(grad_gate)
    o_far = outs.join_far(b_sum)
    b_near = backs.join_near(o_far)
    outs.send_half(b_near)
    grad_up = dot(hold(x_all, b_near), joined([up_grad1, up_grad2]), 0, 0).astype(BF)
    b_far = backs.join_far(grad_up)
    backs.send_half()
    o_part = outs.join_half(b_far)
    backs.join_half(o_part)
    moe_out = outs.rows(slice(0, width), backs.part)

    grad_tokens = backs.rows(slice(0, width))
    prob_all = backs.rows(slice(width, None)).astype(F32)
    grad_prob = jnp.stack(
        [
            jnp.sum(jnp.where(lane == assignment[:, k : k + 1], prob_all, 0.0), axis=1)
            for k in range(assignment.shape[1])
        ],
        axis=1,
    )
    grad_prob = grad_prob / route_weight
    return (moe_out, grad_tokens, grad_prob, grad_gate[None], grad_up[None], grad_down[None])


def solution(mesh):
    return jax.shard_map(
        per_device,
        mesh=mesh,
        in_specs=(
            P("expert", None),
            P("expert", None),
            P("expert", None),
            P("expert", None),
            P("expert", None, "fsdp"),
            P("expert", None, "fsdp"),
            P("expert", "fsdp", None),
        ),
        out_specs=(
            P("expert", None),
            P("expert", None),
            P("expert", None),
            P("expert", None, "fsdp"),
            P("expert", None, "fsdp"),
            P("expert", "fsdp", None),
        ),
        check_vma=False,
    )
```

```python
import jax
import jax.numpy as jnp
from jax import lax
from jax.experimental import pallas as pl
from jax.experimental.pallas import tpu as pltpu
from jax.sharding import PartitionSpec as P

AXES = ("expert", "fsdp")
LANES = 128
BACK_VMEM = 32
EARLY_FLOPS = 60_000_000_000
BF = jnp.bfloat16
F32 = jnp.float32


def log2(size):
    return size.bit_length() - 1


def tile_of(size, most):
    tile = most
    while size % tile:
        tile -= LANES
    return tile


def swap(value, groups, shards, partner):
    pairs = []
    for e in range(groups):
        for f in range(shards):
            to_e, to_f = partner(e, f)
            pairs.append((e * shards + f, to_e * shards + to_f))
    return lax.ppermute(value, AXES, pairs)


class Links:
    def __init__(self):
        self.groups = lax.axis_size("expert")
        self.shards = lax.axis_size("fsdp")
        self.steps = log2(self.groups)
        self.expert = lax.axis_index("expert")
        fsdp = lax.axis_index("fsdp")
        self.core = fsdp % 2
        self.deep = (fsdp // 2) % 2

    def order(self, core):
        return [(k + core) % self.steps for k in range(self.steps)]

    def offsets(self, core):
        found = [0]
        for bit in self.order(core):
            found = found + [o ^ (1 << bit) for o in found]
        return found

    def to_core(self, value):
        return swap(value, self.groups, self.shards, lambda e, f: (e, f ^ 1))

    def to_expert(self, value, step):
        orders = [self.order(0), self.order(1)]
        return swap(
            value, self.groups, self.shards, lambda e, f: (e ^ (1 << orders[f % 2][step]), f)
        )

    def to_offset(self, value, offset):
        return swap(value, self.groups, self.shards, lambda e, f: (e ^ offset, f))

    def to_shard(self, value, bit):
        return swap(value, self.groups, self.shards, lambda e, f: (e, f ^ (1 << bit)))


def add(left, right):
    return (left.astype(F32) + right.astype(F32)).astype(BF)


def hold(value, *others):
    return lax.optimization_barrier((value, *others))[0]


def halves(links, rows, routes=(), weight=0):
    count, width = rows.shape
    quarter, groups = count // 4, links.groups
    extra = LANES if routes else 0
    top = routes[0].shape[1] if routes else 0

    def kernel(*refs):
        inputs, (own_ref, rest_ref) = refs[: 1 + len(routes)], refs[1 + len(routes) :][:2]
        names_ref, weights_ref, sems = refs[-3:]
        fsdp = lax.axis_index("fsdp")
        core, deep = fsdp % 2, (fsdp // 2) % 2
        copies = []
        for source, target in zip(inputs[1:], (names_ref, weights_ref)):
            copies.append((source, target))
        for target, side in ((own_ref, core), (rest_ref, 1 - core)):
            for place, part in enumerate((deep, 1 - deep)):
                start = pl.multiple_of((2 * side + part) * quarter, quarter)
                here = pl.ds(place * quarter, quarter)
                copies.append(
                    (inputs[0].at[pl.ds(start, quarter), :], target.at[here, pl.ds(0, width)])
                )
        copies = [
            pltpu.make_async_copy(source, target, sems.at[k])
            for k, (source, target) in enumerate(copies)
        ]
        for copy in copies:
            copy.start()
        for copy in copies:
            copy.wait()
        if routes:
            source = lax.broadcasted_iota(jnp.int32, (count, count), 1)
            index = lax.broadcasted_iota(jnp.int32, (count, count), 0)
            lane = lax.broadcasted_iota(jnp.int32, (1, LANES), 1)
            for target, side in ((own_ref, core), (rest_ref, 1 - core)):
                place = (index // quarter) % 2
                part = jnp.where(place == 0, deep, 1 - deep)
                wanted = (2 * side + part) * quarter + index % quarter
                left = jnp.zeros((count, LANES), F32)
                for k in range(top):
                    chosen = source == wanted
                    names = jnp.where(chosen, names_ref[k : k + 1, :].astype(F32), 0.0)
                    weights = jnp.where(chosen, weights_ref[k : k + 1, :], 0.0)
                    name = jnp.sum(names, axis=1, keepdims=True)
                    weight = jnp.sum(weights, axis=1, keepdims=True)
                    left += jnp.where(name == (lane % groups).astype(F32), weight, 0.0)
                columns = jnp.zeros_like(left)
                for limb in range(3):
                    high = left.astype(BF).astype(F32)
                    columns = jnp.where(lane // groups == limb, high, columns)
                    left = left - high
                target[:, width:] = columns[: 2 * quarter].astype(BF)

    operands = [rows, *(route.T for route in routes)]
    return pl.pallas_call(
        kernel,
        in_specs=[pl.BlockSpec(memory_space=pltpu.HBM)] * len(operands),
        out_specs=[pl.BlockSpec(memory_space=pltpu.VMEM)] * 2,
        out_shape=[jax.ShapeDtypeStruct((2 * quarter, width + extra), BF)] * 2,
        scratch_shapes=[
            pltpu.VMEM((max(top, 1), count), jnp.int32),
            pltpu.VMEM((max(top, 1), count), F32),
            pltpu.SemaphoreType.DMA((6,)),
        ],
        compiler_params=pltpu.CompilerParams(vmem_limit_bytes=(16 if weight else 60) << 20),
        cost_estimate=pl.CostEstimate(flops=weight, bytes_accessed=0, transcendentals=0),
    )(*operands)


class Rows:
    def __init__(self, links, rows, routes=(), weight=0):
        self.links = links
        self.own, self.rest = halves(links, rows, routes, weight)
        self.came = None
        if links.steps > 1:
            self.came = links.to_expert(self.own, 0)

    def send(self, *after):
        links, held, pieces = self.links, self.own, []
        for step in range(links.steps - 1):
            came = hold(self.came, *after) if step == 0 else links.to_expert(held, step)
            held = jnp.concatenate([held, came], axis=0)
            pieces.append(came)
        self.held = held
        self.last = links.to_expert(self.held, links.steps - 1)
        self.other = links.to_core(jnp.concatenate(pieces, axis=0))

    def first(self, *after):
        return jnp.concatenate([self.held, self.rest, hold(self.other, *after)], axis=0)

    def second(self, *after):
        last = hold(self.last, *after)
        return jnp.concatenate([last, self.links.to_core(last)], axis=0)


def joined(pieces, *after):
    return jnp.concatenate(lax.optimization_barrier((*pieces, *after))[: len(pieces)], axis=0)


class Sum:
    def __init__(self, links):
        self.links = links

    def second(self, terms):
        self.late, self.sent = terms[0], self.links.to_core(terms[1])

    def first(self, terms):
        self.early, self.early_sent = terms[0], self.links.to_core(terms[1])

    def join_second(self, *after):
        self.late = add(self.late, hold(self.sent, *after))
        self.came = self.links.to_expert(self.late, self.links.steps - 1)
        return self.late

    def join_first(self, *after):
        came = hold(self.came, *after)
        total = self.early.astype(F32) + self.early_sent.astype(F32) + came.astype(F32)
        held = total.astype(BF)
        for step in reversed(range(1, self.links.steps - 1)):
            count = held.shape[0] // 2
            held = add(held[:count], self.links.to_expert(held[count:], step))
        count = held.shape[0] // 2
        self.held = held[:count]
        self.came = self.links.to_expert(held[count:], 0)
        return held

    def join_expert(self, *after):
        held = add(self.held, hold(self.came, *after))
        quarter = held.shape[0] // 2
        self.mine = held[:quarter]
        self.came = self.links.to_shard(held[quarter:], 1)
        return held

    def join_near(self, *after):
        self.mine = add(self.mine, hold(self.came, *after))
        self.came = self.links.to_shard(self.mine, 2)
        return self.mine

    def join_far(self, *after):
        self.mine = add(self.mine, hold(self.came, *after))
        for bit in range(3, log2(self.links.shards)):
            self.mine = add(self.mine, self.links.to_shard(self.mine, bit))
        return self.mine

    def send_half(self, *after):
        self.came = self.links.to_shard(hold(self.mine, *after), 1)

    def join_half(self, *after):
        beside = hold(self.came, *after)
        self.part = jnp.where(
            self.links.deep == 0,
            jnp.concatenate([self.mine, beside], axis=0),
            jnp.concatenate([beside, self.mine], axis=0),
        )
        self.came = self.links.to_core(self.part)
        return self.part

    def rows(self, columns, *after):
        part, other = self.part[:, columns], hold(self.came, *after)[:, columns]
        both = lax.optimization_barrier(jnp.concatenate([part, part], axis=0))
        start = (1 - self.links.core) * part.shape[0]
        return lax.dynamic_update_slice_in_dim(both, other, start, 0)


def dot(left, right, left_dim, right_dim):
    return lax.dot_general(
        left, right, (((left_dim,), (right_dim,)), ((), ())), preferred_element_type=F32
    )


def front(rows, gate, up, *after):
    pre_gate = dot(rows, gate, 1, 0)
    pre_up = dot(hold(rows, pre_gate, *after), up, 1, 0)
    sigma = jax.nn.sigmoid(pre_gate)
    silu = pre_gate * sigma
    hidden = (silu * pre_up).astype(BF)
    slope = (pre_up * sigma * (1.0 + pre_gate * (1.0 - sigma))).astype(BF)
    return lax.optimization_barrier((hidden, slope, silu.astype(BF), pre_up.astype(BF)))


def hidden_grads(rows, down, slope, silu, weight):
    raw = dot(rows, down, 1, 1) * weight
    return lax.optimization_barrier(
        ((raw * slope.astype(F32)).astype(BF), (raw * silu.astype(F32)).astype(BF))
    )


def out_terms(hidden, down, weight):
    middle = hidden.shape[0] // 2
    term = (dot(hidden, down, 1, 0) * weight).astype(BF)
    return term[:middle], term[middle:]


def back_terms(grad_gate, grad_up, pre_up, gate, up):
    rows, units, width = grad_gate.shape[0], gate.shape[1], gate.shape[0]
    tile = tile_of(width, 768)
    tiles = width // tile
    middle = rows // 2
    nt = (((1,), (1,)), ((), ()))

    def kernel(gate_grad, up_grad, pre_ref, gate_ref, up_ref, keep_ref, send_ref):
        j = pl.program_id(0)
        term = lax.dot_general(gate_grad[...], gate_ref[...], nt, preferred_element_type=F32)
        term += lax.dot_general(up_grad[...], up_ref[...], nt, preferred_element_type=F32)
        term = term.astype(BF)
        columns = pl.ds(pl.multiple_of(j * tile, LANES), tile)
        keep_ref[:, columns] = term[:middle]
        send_ref[:, columns] = term[middle:]

        @pl.when(j == tiles - 1)
        def _():
            lane = lax.broadcasted_iota(jnp.int32, (rows, LANES), 1)
            prob = jnp.sum(
                up_grad[...].astype(F32) * pre_ref[...].astype(F32), axis=1, keepdims=True
            )
            own = jnp.where(lane == lax.axis_index("expert"), prob, 0.0).astype(BF)
            keep_ref[:, width:] = own[:middle]
            send_ref[:, width:] = own[middle:]

    block = pl.BlockSpec((middle, width + LANES), lambda j: (0, 0))
    full = pl.BlockSpec((rows, units), lambda j: (0, 0))
    row = pl.BlockSpec((tile, units), lambda j: (j, 0))
    return pl.pallas_call(
        kernel,
        grid=(tiles,),
        in_specs=[full] * 3 + [row] * 2,
        out_specs=[block] * 2,
        out_shape=[jax.ShapeDtypeStruct((middle, width + LANES), BF)] * 2,
        compiler_params=pltpu.CompilerParams(vmem_limit_bytes=24 << 20),
        cost_estimate=pl.CostEstimate(flops=0, bytes_accessed=0, transcendentals=0),
    )(grad_gate, grad_up, pre_up, gate, up)


def per_device(tokens, assignment, route_weight, cotangent, w_gate, w_up, w_down):
    links = Links()
    width = tokens.shape[1]
    gate, up, down = w_gate[0], w_up[0], w_down[0]
    lane = lax.broadcasted_iota(jnp.int32, (1, LANES), 1)

    x = Rows(links, tokens, (assignment, route_weight))
    c = Rows(links, hold(cotangent, x.own), weight=EARLY_FLOPS)

    def weights(chunk):
        own = jnp.logical_and(lane % links.groups == links.expert, lane < 3 * links.groups)
        limbs = jnp.where(own, chunk[:, width:].astype(F32), 0.0)
        return jnp.sum(limbs, axis=1, keepdims=True)

    outs, backs = Sum(links), Sum(links)
    x.send()
    x1 = x.first()
    hidden1, slope1, silu1, up1 = front(x1[:, :width], gate, up, c.came)
    weight1 = weights(x1)
    c.send(x1)
    c1 = c.first()
    gate_grad1, up_grad1 = hidden_grads(c1, down, slope1, silu1, weight1)
    x2 = x.second()
    x2 = hold(x2, gate_grad1)
    hidden2, slope2, silu2, up2 = front(x2[:, :width], gate, up)
    weight2 = weights(x2)
    out2 = lax.optimization_barrier(out_terms(hidden2, down, weight2))
    outs.second(out2)
    out1 = lax.optimization_barrier(out_terms(hold(hidden1, *out2), down, weight1))
    outs.first(out1)
    o_late = outs.join_second(*out1)
    c2 = c.second(hidden2)
    gate_grad2, up_grad2 = hidden_grads(hold(c2, o_late), down, slope2, silu2, weight2)
    back2 = back_terms(gate_grad2, up_grad2, up2, gate, up)
    backs.second(back2)
    o_held = outs.join_first(*back2)
    back1 = back_terms(hold(gate_grad1, o_held), up_grad1, up1, gate, up)
    backs.first(back1)
    b_late = backs.join_second(*back1)
    weight = jnp.concatenate([weight1, weight2], axis=0)
    o_sum = outs.join_expert(b_late)
    scaled = (joined([hidden1, hidden2], o_sum).astype(F32) * weight).astype(BF)
    grad_down = dot(scaled, joined([c1, c2], o_sum), 0, 0).astype(BF)
    o_near = outs.join_near(grad_down)
    b_held = backs.join_first(o_near)
    x_all = joined([x1, x2], b_held)[:, :width]
    grad_gate = dot(x_all, joined([gate_grad1, gate_grad2]), 0, 0).astype(BF)
    b_sum = backs.join_expert(grad_gate)
    o_far = outs.join_far(b_sum)
    b_near = backs.join_near(o_far)
    outs.send_half(b_near)
    grad_up = dot(hold(x_all, b_near), joined([up_grad1, up_grad2]), 0, 0).astype(BF)
    b_far = backs.join_far(grad_up)
    backs.send_half()
    o_part = outs.join_half(b_far)
    backs.join_half(o_part)
    moe_out = outs.rows(slice(0, width), backs.part)

    grad_tokens = backs.rows(slice(0, width))
    prob_all = backs.rows(slice(width, None)).astype(F32)
    grad_prob = jnp.stack(
        [
            jnp.sum(jnp.where(lane == assignment[:, k : k + 1], prob_all, 0.0), axis=1)
            for k in range(assignment.shape[1])
        ],
        axis=1,
    )
    grad_prob = grad_prob / route_weight
    return (moe_out, grad_tokens, grad_prob, grad_gate[None], grad_up[None], grad_down[None])


def solution(mesh):
    return jax.shard_map(
        per_device,
        mesh=mesh,
        in_specs=(
            P("expert", None),
            P("expert", None),
            P("expert", None),
            P("expert", None),
            P("expert", None, "fsdp"),
            P("expert", None, "fsdp"),
            P("expert", "fsdp", None),
        ),
        out_specs=(
            P("expert", None),
            P("expert", None),
            P("expert", None),
            P("expert", None, "fsdp"),
            P("expert", None, "fsdp"),
            P("expert", "fsdp", None),
        ),
        check_vma=False,
    )
```
